32 devices in a mesh: groups: 2 (over y), particle: 4 (over z), head: 4 (over x, core).
Axes of the slice: x: 2, y: 2, z: 4, core: 2. Of those that a mesh axis runs over, the one named last changes fastest.
Arguments:
- tokens: int32 [64, 8], P(('groups', 'particle')), parts along dimension 0, may hold values from 0 to 64127
- ancestors: int32 [64], P(('groups', 'particle')), parts along dimension 0, may hold values from 0 to 31, as said below
- embedding: bfloat16 [64128, 4096], P('particle', 'head'), may hold values from -6 to 6
- norm_gain: bfloat16 [4096], replicated, may hold values from 0.099609375 to 1.8984375
- w_query: bfloat16 [4096, 4096], P(None, 'head'), may hold values from -0.09375 to 0.09375
- w_key: bfloat16 [4096, 1024], P(None, 'head'), may hold values from -0.09375 to 0.09375
- w_value: bfloat16 [4096, 1024], P(None, 'head'), may hold values from -0.5 to 0.5
- key_cache: bfloat16 [64, 8, 256, 128], P(('groups', 'particle'), 'head'), parts along dimension 0, may hold values from -200 to 200
- value_cache: bfloat16 [64, 8, 256, 128], P(('groups', 'particle'), 'head'), parts along dimension 0, may hold values from -6 to 6
Outputs:
- block_output: bfloat16 [64, 8, 4096], P(('groups', 'particle'), None, 'head'), parts along dimension 0
The draws below stay inside these ranges and needn't reach their ends.
There are 2 independent parts, one for each index of `groups`. The reference program is written for one: setup_inputs(seed, part) draws one part's arguments, and reference() takes and returns one part's arrays. A program takes and returns all parts, laid end to end along the dimension named above; an argument that names none is the same for every part. Nothing has to cross between parts.
Inputs may be any that keep to these rules, and one draw needn't show every extreme that they name: ancestors never fall from one particle to the next; particle 0 descends from 0 and particle 32 - 1 from 31.
All inputs are finite; a program needn't handle non-finite values.
Results may differ from the reference program's by a relative error of at most 0.011.
Values may be sent and summed in bfloat16 or wider, within the bound.
A program may use at most 128 MiB of HBM per device.

```python
import math
import jax
import jax.numpy as jnp
import numpy as np
from jax import lax

D = 4096
QH = 32
KVH = 8
HEAD_DIM = 128
VOCAB = 64128
STEPS = 8
CTX = 256
P_TOTAL = 32


def draw_ancestors(key, part):
    key = jax.random.fold_in(key, 11)
    weight_key, offset_key, leader_key = jax.random.split(key, 3)
    levels = jax.random.randint(weight_key, (P_TOTAL,), 0, 8)
    base_weights = 1 + levels * levels * levels
    leader = jax.random.randint(leader_key, (), P_TOTAL // 4, 3 * P_TOTAL // 4)
    positions = jnp.arange(P_TOTAL, dtype=jnp.int32)
    leader_weight = jnp.sum(base_weights) - jnp.sum(jnp.where(positions == leader, base_weights, 0))
    weights = jnp.where(positions == leader, leader_weight, base_weights)
    bounds = jnp.cumsum(weights) * P_TOTAL
    weight_sum = jnp.sum(weights)
    offset = jax.random.randint(offset_key, (), 0, weight_sum)
    targets = positions * weight_sum + offset
    parents = jnp.sum((bounds[None, :] <= targets[:, None]).astype(jnp.int32), axis=1)
    parents = jnp.where(positions == 0, 0, parents)
    parents = jnp.where(positions == P_TOTAL - 1, P_TOTAL - 1, parents)
    return parents.astype(jnp.int32)


def draw_key_cache(key, part):
    key = jax.random.fold_in(key, 23)
    background_key = jax.random.fold_in(key, 0)
    cache_shape = (P_TOTAL, KVH, CTX, HEAD_DIM)
    drawn_keys = jax.random.normal(background_key, cache_shape, jnp.float32)
    return drawn_keys.astype(jnp.bfloat16)


def set_ends(result, own_key, low, top_value):
    longest = result.shape.index(max(result.shape))
    spots = []
    for shift in (0, 1):
        where = [jax.random.randint(jax.random.fold_in(own_key, axis), (), 0, length) for axis, length in enumerate(result.shape)]
        where[longest] = (where[longest] + shift) % result.shape[longest]
        spots.append(tuple(where))
    return result.at[spots[0]].set(low).at[spots[1]].set(top_value)


def block_levels(stream_key, dims, cuts, least, high):
    loudness = 1.0
    for position, parts in cuts:
        draws = jax.random.uniform(jax.random.fold_in(jax.random.fold_in(stream_key, 6), position), (parts,), jnp.float32, least / len(cuts), high / len(cuts))
        loudness = loudness * jnp.repeat(jnp.exp(draws), dims[position] // parts).reshape((-1,) + (1,) * (len(dims) - 1 - position))
    return loudness


def rank_table(amount, skew):
    portions = [(1 << 20) // math.isqrt(standing ** skew) + 1 for standing in range(1, amount + 1)]
    deviation = 1 + sum(portions) // (1 << 30)
    return np.cumsum(np.array([max(1, weight // deviation) for weight in portions]))


def ranked_ids(stream_key, dims, count, skew):
    listing = rank_table(count, skew)
    lot = jax.random.randint(jax.random.fold_in(stream_key, 1), dims, 0, int(listing[count - 1]))
    standing = jnp.searchsorted(jnp.asarray(listing, jnp.int32), lot, side="right")
    return jax.random.permutation(jax.random.fold_in(stream_key, 2), count)[standing].astype(jnp.int32)


def scatter_about(stream_key, extent, deviation, most, cuts=(), kind=jnp.bfloat16):
    factor_of = block_levels(stream_key, extent, cuts, -0.22, 0.18) if cuts else 1.0
    drawn = jax.random.normal(stream_key, extent, jnp.float32) * deviation * factor_of
    return jnp.minimum(jnp.maximum(drawn, -most), most).astype(kind)


def setup_inputs(seed: int = 0, part: int = 0) -> dict:
    streams_of = jax.random.split(jax.random.key(seed), 10)
    part_splits = jax.random.split(jax.random.fold_in(streams_of[9], part), 10)
    tokens = set_ends(ranked_ids(part_splits[0], (P_TOTAL, STEPS), VOCAB, 2), jax.random.fold_in(part_splits[0], 3), 0, VOCAB - 1).astype(jnp.int32)
    ancestors = draw_ancestors(jax.random.fold_in(jax.random.fold_in(streams_of[9], part), 71), part)
    embedding = scatter_about(streams_of[2], (VOCAB, D), 1.0, 6.0, ((0, 4), (1, 4)))
    norm_gain = jnp.clip(1.0 + 0.18 * jax.random.normal(streams_of[3], (D,), jnp.float32), 0.099609375, 1.8984375).astype(jnp.bfloat16)
    w_query = scatter_about(streams_of[4], (D, QH * HEAD_DIM), D ** -0.5, 0.09375, ((1, 4),))
    w_key = scatter_about(streams_of[5], (D, KVH * HEAD_DIM), D ** -0.5, 0.09375, ((1, 4),))
    w_value = scatter_about(streams_of[6], (D, KVH * HEAD_DIM), HEAD_DIM ** -0.5, 0.5, ((1, 4),))
    key_cache = draw_key_cache(jax.random.fold_in(jax.random.fold_in(streams_of[9], part), 71), part)
    value_cache = scatter_about(part_splits[8], (P_TOTAL, KVH, CTX, HEAD_DIM), 1.0, 6.0, ((0, 4), (1, 4)))
    return dict(tokens=tokens, ancestors=ancestors, embedding=embedding, norm_gain=norm_gain, w_query=w_query, w_key=w_key, w_value=w_value, key_cache=key_cache, value_cache=value_cache)


def angles(step_count, head_size, first_position):
    half_size = head_size // 2
    freqs = 500000.0 ** (-(2.0 * jnp.arange(half_size, dtype=jnp.float32)) / head_size)
    positions = (first_position + jnp.arange(step_count)).astype(jnp.float32)
    phase = positions[:, None] * freqs[None, :]
    return (jnp.cos(phase), jnp.sin(phase))

def rotate(values, cosine_table, sine_table):
    half_size = values.shape[-1] // 2
    front_half = values[..., :half_size]
    back_half = values[..., half_size:]
    return jnp.concatenate([front_half * cosine_table - back_half * sine_table, back_half * cosine_table + front_half * sine_table], axis=-1)

def reference(tokens, ancestors, embedding, norm_gain, w_query, w_key, w_value, key_cache, value_cache):
    particles = tokens.shape[0]
    group_size = QH // KVH
    score_scale = 1.0 / math.sqrt(HEAD_DIM)
    embedded = embedding[tokens.reshape(-1)].astype(jnp.float32)
    mean_square = lax.optimization_barrier(jnp.mean(embedded * embedded, axis=-1, keepdims=True))
    normed = (embedded * lax.rsqrt(mean_square + 1e-05) * norm_gain.astype(jnp.float32)).astype(jnp.bfloat16)
    cosine_table, sine_table = angles(STEPS, HEAD_DIM, CTX)
    queries = jnp.dot(normed, w_query, preferred_element_type=jnp.float32).reshape(particles, STEPS, KVH, group_size, HEAD_DIM)
    queries = rotate(queries, cosine_table[None, :, None, None, :], sine_table[None, :, None, None, :]).astype(jnp.bfloat16)
    new_keys = jnp.dot(normed, w_key, preferred_element_type=jnp.float32).reshape(particles, STEPS, KVH, HEAD_DIM)
    new_keys = rotate(new_keys, cosine_table[None, :, None, :], sine_table[None, :, None, :]).astype(jnp.bfloat16)
    new_values = jnp.dot(normed, w_value, preferred_element_type=jnp.float32).reshape(particles, STEPS, KVH, HEAD_DIM).astype(jnp.bfloat16)
    causal = jnp.arange(STEPS)[:, None] >= jnp.arange(STEPS)[None, :]

    def attend_one(member):
        query_rows, key_rows, value_rows, parent = member
        cached_keys = lax.dynamic_index_in_dim(key_cache, parent, 0, keepdims=False).astype(jnp.float32)
        cached_values = lax.dynamic_index_in_dim(value_cache, parent, 0, keepdims=False).astype(jnp.float32)
        query_float = query_rows.astype(jnp.float32)
        cache_scores = jnp.einsum('skgd,ktd->skgt', query_float, cached_keys) * score_scale
        own_scores = jnp.einsum('skgd,rkd->skgr', query_float, key_rows.astype(jnp.float32)) * score_scale
        own_scores = jnp.where(causal[:, None, None, :], own_scores, -jnp.inf)
        highest = jnp.maximum(lax.optimization_barrier(jnp.max(cache_scores, axis=-1)), lax.optimization_barrier(jnp.max(own_scores, axis=-1)))
        cache_weights = jnp.exp(cache_scores - highest[..., None])
        own_weights = jnp.exp(own_scores - highest[..., None])
        denominator = lax.optimization_barrier(jnp.sum(cache_weights, axis=-1)) + lax.optimization_barrier(jnp.sum(own_weights, axis=-1))
        accumulated = jnp.einsum('skgt,ktd->skgd', cache_weights, cached_values)
        accumulated = accumulated + jnp.einsum('skgr,rkd->skgd', own_weights, value_rows.astype(jnp.float32))
        return (accumulated / denominator[..., None]).astype(jnp.bfloat16)
    attended = lax.map(attend_one, (queries, new_keys, new_values, ancestors))
    return attended.reshape(particles, STEPS, QH * HEAD_DIM)
```

```python
import functools
import math

import jax
import jax.numpy as jnp
import numpy as np
from jax import lax
from jax.experimental import pallas as pl
from jax.experimental.pallas import tpu as pltpu
from jax.sharding import PartitionSpec as P

MESH = pl.DeviceIdType.MESH
VMEM_LIMIT = 48 * 1024 * 1024


def remote(src, dst, send_sem, recv_sem, **where):
    return pltpu.make_async_remote_copy(
        src_ref=src,
        dst_ref=dst,
        send_sem=send_sem,
        recv_sem=recv_sem,
        device_id=where,
        device_id_type=MESH,
    )


def ids_kernel(n, ids_ref, all_ref, send_sem, recv_sem):
    me = lax.axis_index("particle")
    peers = [lax.rem(me + r, n) for r in range(1, n)]
    barrier = pltpu.get_barrier_semaphore()
    for peer in peers:
        pl.semaphore_signal(barrier, inc=1, device_id={"particle": peer}, device_id_type=MESH)
    pl.semaphore_wait(barrier, n - 1)
    copies = [
        remote(ids_ref, all_ref.at[me], send_sem.at[r], recv_sem.at[r], particle=peer)
        for r, peer in enumerate(peers)
    ]
    for copy in copies:
        copy.start()
    all_ref[me] = ids_ref[...]
    for copy in copies:
        copy.wait()


def rows_kernel(n, particles, steps, tile, ids_ref, table_ref, out_ref, blocks, found, listed, sem):
    vocab_rows = table_ref.shape[0]
    first = lax.axis_index("particle") * vocab_rows
    per_device = particles * steps

    def look(member, count):
        owner = member // particles
        child = lax.rem(member, particles)
        for step in range(steps):
            local = ids_ref[owner, child, step] - first
            token = member * steps + step
            owned = jnp.logical_and(local >= 0, local < vocab_rows)
            listed[0, count] = token
            listed[1, count] = local

            @pl.when(owned)
            def _():
                start = pl.multiple_of((local // tile) * tile, tile)
                pltpu.make_async_copy(
                    table_ref.at[pl.ds(start, tile)], blocks.at[count], sem
                ).start()

            count = count + owned.astype(jnp.int32)
        return count

    found[...] = jnp.zeros_like(found)
    count = lax.fori_loop(0, n * particles, look, 0)

    def arrive(slot, carry):
        pltpu.make_async_copy(table_ref.at[pl.ds(0, tile)], blocks.at[slot], sem).wait()
        return carry

    lax.fori_loop(0, count, arrive, 0)

    def pick(slot, carry):
        token, local = listed[0, slot], listed[1, slot]
        row = lax.rem(local, tile)
        block = blocks[slot].astype(jnp.float32)
        here = lax.broadcasted_iota(jnp.int32, block.shape, 0) == row
        found[pl.ds(token, 1), :] = jnp.sum(jnp.where(here, block, 0.0), axis=0, keepdims=True)
        return carry

    lax.fori_loop(0, count, pick, 0)
    out_ref[...] = found[...].astype(out_ref.dtype)


def main_kernel(
    n,
    heads,
    deltas,
    widths,
    ids_ref,
    rows_ref,
    gain_ref,
    cos_ref,
    sin_ref,
    wq_hbm,
    wk_hbm,
    wv_hbm,
    kc_hbm,
    vc_hbm,
    out_ref,
    wq,
    wk,
    wv,
    kc,
    vc,
    came,
    emb,
    proj,
    query,
    new_k,
    new_v,
    q_in,
    res_out,
    lse_out,
    res_in,
    lse_in,
    own_res,
    load_sem,
    a_send,
    a_recv,
    x_send,
    x_recv,
    s_send,
    s_recv,
    q_send,
    q_recv,
    r_send,
    r_recv,
    l_send,
    l_recv,
):
    particles, kv = kc.shape[0], kc.shape[1]
    steps = cos_ref.shape[0]
    head_size = kc.shape[3]
    tokens = particles * steps
    local_heads = wq.shape[1] // head_size
    group = local_heads // kv
    rows = group * steps
    depth = rows_ref.shape[1]
    scale = 1.0 / math.sqrt(head_size)
    z = lax.axis_index("particle")
    h = lax.axis_index("head")
    cores = 2
    chips = heads // cores
    chip, core = h // cores, lax.rem(h, cores)
    sibling = chip * cores + 1 - core

    loads = [
        pltpu.make_async_copy(src, dst, load_sem.at[i])
        for i, (src, dst) in enumerate(
            ((wq_hbm, wq), (wk_hbm, wk), (wv_hbm, wv), (kc_hbm, kc), (vc_hbm, vc))
        )
    ]
    for load in loads:
        load.start()

    z_peers = [lax.rem(z + r, n) for r in range(1, n)]
    x_peers = [lax.rem(chip + r, chips) * cores + core for r in range(1, chips)]
    x_from = [lax.rem(chip - r + chips, chips) * cores + core for r in range(1, chips)]
    barrier = pltpu.get_barrier_semaphore()
    for peer in z_peers:
        pl.semaphore_signal(barrier, inc=1, device_id={"particle": peer}, device_id_type=MESH)
    for peer in x_peers + [sibling]:
        pl.semaphore_signal(barrier, inc=1, device_id={"head": peer}, device_id_type=MESH)
    pl.semaphore_wait(barrier, n - 1 + chips)

    a_copies = [
        remote(
            rows_ref.at[pl.ds(pl.multiple_of(peer * tokens, tokens), tokens)],
            came.at[r],
            a_send.at[r],
            a_recv.at[r],
            particle=peer,
        )
        for r, peer in enumerate(z_peers)
    ]
    for copy in a_copies:
        copy.start()
    total = rows_ref[pl.ds(pl.multiple_of(z * tokens, tokens), tokens), :]
    for r, copy in enumerate(a_copies):
        copy.wait_recv()
        total = total + came[r]
    emb[h] = total

    sib_own = remote(emb.at[h], emb.at[h], s_send.at[0], s_recv.at[0], head=sibling)
    x_copies = [
        remote(emb.at[h], emb.at[h], x_send.at[r], x_recv.at[r], head=peer)
        for r, peer in enumerate(x_peers)
    ]
    for copy in x_copies:
        copy.start()
    sib_own.start()
    for load in loads[:3]:
        load.wait()

    square = jnp.zeros((tokens, 1), jnp.float32)

    def contract(square, index, first):
        part = emb[index].astype(jnp.float32)
        square = square + jnp.sum(part * part, axis=1, keepdims=True)
        at = pl.ds(pl.multiple_of(index * depth, depth), depth)
        scaled = (part * gain_ref[:, at].astype(jnp.float32)).astype(jnp.bfloat16)
        column = 0
        for weight in (wq, wk, wv):
            for begin in range(0, weight.shape[1], 128 if weight.shape[1] % 256 else 256):
                width = 128 if weight.shape[1] % 256 else 256
                product = jnp.dot(
                    scaled,
                    weight[at, begin : begin + width],
                    preferred_element_type=jnp.float32,
                )
                where = slice(column, column + width)
                if first:
                    proj[:, where] = product
                else:
                    proj[:, where] += product
                column += width
        return square

    square = contract(square, h, True)
    sib_own.wait_recv()
    square = contract(square, sibling, False)
    forwards = []
    for r, (copy, source) in enumerate(zip(x_copies, x_from)):
        copy.wait_recv()
        forward = remote(
            emb.at[source], emb.at[source], s_send.at[r + 1], s_recv.at[r + 1], head=sibling
        )
        forward.start()
        forwards.append(forward)
        square = contract(square, source, False)
    for r, forward in enumerate(forwards):
        forward.wait_recv()
        source = lax.rem(chip - (r + 1) + chips, chips) * cores + 1 - core
        square = contract(square, source, False)

    norm = lax.rsqrt(square * (1.0 / (depth * heads)) + 1e-5)
    cosine, sine = cos_ref[...], sin_ref[...]

    def spin(column):
        value = proj[:, column * head_size : (column + 1) * head_size] * norm
        turned = pltpu.roll(value, head_size // 2, 1)
        shape = (particles, steps, head_size)
        return value.reshape(shape) * cosine[None] + turned.reshape(shape) * sine[None]

    for k in range(kv):
        for pair in range(0, group, 2):
            both = jnp.concatenate([spin(k * group + pair), spin(k * group + pair + 1)], axis=1)
            query[:, k, pair * steps : (pair + 2) * steps, :] = both.astype(jnp.bfloat16)

    def span(d):
        width = widths[abs(d)]
        return (0 if d < 0 else particles - width), width

    def reaches(d):
        return jnp.logical_and(z + d >= 0, z + d < n)

    def query_copy(i, d):
        begin, width = span(d)
        return remote(
            query.at[pl.ds(begin, width)],
            q_in.at[i, pl.ds(begin, width)],
            q_send.at[i],
            q_recv.at[i],
            particle=z + d,
        )

    def back_copies(i, d):
        begin, width = span(d)
        return (
            remote(
                res_out.at[i, pl.ds(begin, width)],
                res_in.at[i, pl.ds(begin, width)],
                r_send.at[i],
                r_recv.at[i],
                particle=z - d,
            ),
            remote(
                lse_out.at[i], lse_in.at[i], l_send.at[i], l_recv.at[i], particle=z - d
            ),
        )

    for i, d in enumerate(deltas):

        @pl.when(reaches(d))
        def _():
            query_copy(i, d).start()

    for k in range(kv):
        new_k[k] = spin(local_heads + k).reshape(tokens, head_size).astype(jnp.bfloat16)
        base = (local_heads + kv + k) * head_size
        new_v[k] = (proj[:, base : base + head_size] * norm).astype(jnp.bfloat16)

    own_lse = []
    for k in range(kv):
        q_rows = query[:, k].reshape(particles * rows, head_size)
        scores = lax.dot_general(
            q_rows, new_k[k], (((1,), (1,)), ((), ())), preferred_element_type=jnp.float32
        ) * scale
        at_row = lax.broadcasted_iota(jnp.int32, scores.shape, 0)
        at_key = lax.broadcasted_iota(jnp.int32, scores.shape, 1)
        seen = jnp.logical_and(
            at_row // rows == at_key // steps,
            lax.rem(at_key, steps) <= lax.rem(at_row, steps),
        )
        scores = jnp.where(seen, scores, -1e30)
        top = jnp.max(scores, axis=1, keepdims=True)
        weight = jnp.exp(scores - top)
        weight = jnp.where(seen, weight, 0.0)
        amount = jnp.sum(weight, axis=1, keepdims=True)
        summed = jnp.dot(weight.astype(jnp.bfloat16), new_v[k], preferred_element_type=jnp.float32)
        own_res[k] = summed / amount
        own_lse.append(top + jnp.log(amount))

    for load in loads[3:]:
        load.wait()

    lane = lax.broadcasted_iota(jnp.int32, (rows, 128), 1)

    def attend(i, source_query, begin, width, source):
        some = 4 if width % 4 == 0 else 1

        def some_children(block, lse):
            for offset in range(some):
                child = begin + block * some + offset
                parent = ids_ref[source, child, steps] - z * particles
                parent = jnp.minimum(jnp.maximum(parent, 0), particles - 1)
                for k in range(kv):
                    scores = lax.dot_general(
                        source_query(child, k),
                        kc[parent, k],
                        (((1,), (1,)), ((), ())),
                        preferred_element_type=jnp.float32,
                    ) * scale
                    top = jnp.max(scores, axis=1, keepdims=True)
                    weight = jnp.exp(scores - top)
                    amount = jnp.sum(weight, axis=1, keepdims=True)
                    summed = jnp.dot(
                        weight.astype(jnp.bfloat16),
                        vc[parent, k],
                        preferred_element_type=jnp.float32,
                    )
                    res_out[i, child, k] = (summed / amount).astype(jnp.bfloat16)
                    lse = jnp.where(lane == child * kv + k, top + jnp.log(amount), lse)
            return lse

        lse_out[i] = lax.fori_loop(
            0, width // some, some_children, jnp.zeros((rows, 128), jnp.float32)
        )

    own = len(deltas)
    attend(own, lambda child, k: query[child, k], 0, particles, z)
    res_in[own] = res_out[own]
    lse_in[own] = lse_out[own]

    for i, d in enumerate(deltas):

        @pl.when(reaches(-d))
        def _():
            query_copy(i, d).wait_recv()
            begin, width = span(d)
            attend(i, lambda child, k: q_in[i, child, k], begin, width, z - d)
            for copy in back_copies(i, d):
                copy.start()

    for i, d in enumerate(deltas):

        @pl.when(reaches(d))
        def _():
            for copy in back_copies(i, d):
                copy.wait_recv()

    for child in range(particles):
        owner = ids_ref[z, child, steps] // particles
        slot = jnp.int32(own)
        for i, d in enumerate(deltas):
            slot = jnp.where(owner - z == d, i, slot)
        parts = []
        lse_tile = lse_in[slot]
        for k in range(kv):
            cached = res_in[slot, child, k].astype(jnp.float32)
            cached_lse = jnp.sum(
                jnp.where(lane == child * kv + k, lse_tile, 0.0), axis=1, keepdims=True
            )
            at = slice(child * rows, (child + 1) * rows)
            mine, mine_lse = own_res[k, at, :], own_lse[k][at, :]
            top = jnp.maximum(cached_lse, mine_lse)
            cached_factor = jnp.exp(cached_lse - top)
            mine_factor = jnp.exp(mine_lse - top)
            mixed = (cached * cached_factor + mine * mine_factor) / (cached_factor + mine_factor)
            for g in range(group):
                parts.append(mixed[g * steps : (g + 1) * steps, :])
        out_ref[child] = jnp.concatenate(parts, axis=1).astype(out_ref.dtype)

    for copy in a_copies + x_copies + forwards + [sib_own]:
        copy.wait_send()
    for i, d in enumerate(deltas):

        @pl.when(reaches(d))
        def _():
            query_copy(i, d).wait_send()

        @pl.when(reaches(-d))
        def _():
            for copy in back_copies(i, d):
                copy.wait_send()


def tables(steps, head_size, first_position):
    half = head_size // 2
    freqs = 500000.0 ** (-(2.0 * np.arange(half)) / head_size)
    phase = (first_position + np.arange(steps))[:, None] * freqs[None, :]
    cosine, sine = np.cos(phase), np.sin(phase)
    return (
        np.concatenate([cosine, cosine], axis=1).astype(np.float32),
        np.concatenate([-sine, sine], axis=1).astype(np.float32),
    )


def per_device(
    n,
    heads,
    tokens,
    ancestors,
    embedding,
    norm_gain,
    w_query,
    w_key,
    w_value,
    key_cache,
    value_cache,
):
    particles, steps = tokens.shape
    _, kv, context, head_size = key_cache.shape
    local_heads = w_query.shape[1] // head_size
    vocab_rows, depth = embedding.shape
    count = particles * steps
    rows = local_heads // kv * steps
    vmem = pl.BlockSpec(memory_space=pltpu.VMEM)
    smem = pl.BlockSpec(memory_space=pltpu.SMEM)
    hbm = pl.BlockSpec(memory_space=pl.ANY)
    dma = pltpu.SemaphoreType.DMA

    ids = jnp.concatenate([tokens, ancestors[:, None]], axis=1)
    ids = jnp.pad(ids, ((0, 0), (0, 128 - ids.shape[1])))
    all_ids = pl.pallas_call(
        functools.partial(ids_kernel, n),
        out_shape=jax.ShapeDtypeStruct((n, particles, 128), jnp.int32),
        in_specs=[vmem],
        out_specs=vmem,
        scratch_shapes=[dma((n - 1,)), dma((n - 1,))],
        compiler_params=pltpu.CompilerParams(collective_id=0, has_side_effects=True),
    )(ids)

    tile = 16 if vocab_rows % 16 == 0 else 8
    owned = pl.pallas_call(
        functools.partial(rows_kernel, n, particles, steps, tile),
        out_shape=jax.ShapeDtypeStruct((n * count, depth), jnp.bfloat16),
        in_specs=[smem, hbm],
        out_specs=vmem,
        scratch_shapes=[
            pltpu.VMEM((n * count, tile, depth), jnp.bfloat16),
            pltpu.VMEM((n * count, depth), jnp.float32),
            pltpu.SMEM((2, n * count + 1), jnp.int32),
            dma,
        ],
        compiler_params=pltpu.CompilerParams(vmem_limit_bytes=VMEM_LIMIT),
    )(all_ids, embedding)

    deltas = [d for r in range(1, n) for d in (r, -r)]
    widths = {r: particles for r in range(1, n)}
    slots = len(deltas)
    chips = heads // 2
    cosine, sine = tables(steps, head_size, context)
    bf16, f32 = jnp.bfloat16, jnp.float32
    return pl.pallas_call(
        functools.partial(main_kernel, n, heads, deltas, widths),
        out_shape=jax.ShapeDtypeStruct((particles, steps, local_heads * head_size), bf16),
        in_specs=[smem] + [vmem] * 4 + [hbm] * 5,
        out_specs=vmem,
        scratch_shapes=[
            pltpu.VMEM(w_query.shape, bf16),
            pltpu.VMEM(w_key.shape, bf16),
            pltpu.VMEM(w_value.shape, bf16),
            pltpu.VMEM(key_cache.shape, bf16),
            pltpu.VMEM(value_cache.shape, bf16),
            pltpu.VMEM((n - 1, count, depth), bf16),
            pltpu.VMEM((heads, count, depth), bf16),
            pltpu.VMEM((count, (local_heads + 2 * kv) * head_size), f32),
            pltpu.VMEM((particles, kv, rows, head_size), bf16),
            pltpu.VMEM((kv, count, head_size), bf16),
            pltpu.VMEM((kv, count, head_size), bf16),
            pltpu.VMEM((slots, particles, kv, rows, head_size), bf16),
            pltpu.VMEM((slots + 1, particles, kv, rows, head_size), bf16),
            pltpu.VMEM((slots + 1, rows, 128), f32),
            pltpu.VMEM((slots + 1, particles, kv, rows, head_size), bf16),
            pltpu.VMEM((slots + 1, rows, 128), f32),
            pltpu.VMEM((kv, particles * rows, head_size), f32),
            dma((5,)),
            dma((n - 1,)),
            dma((n - 1,)),
            dma((max(chips - 1, 1),)),
            dma((max(chips - 1, 1),)),
            dma((chips,)),
            dma((chips,)),
            dma((slots,)),
            dma((slots,)),
            dma((slots,)),
            dma((slots,)),
            dma((slots,)),
            dma((slots,)),
        ],
        compiler_params=pltpu.CompilerParams(
            collective_id=1, has_side_effects=True, vmem_limit_bytes=VMEM_LIMIT
        ),
    )(
        all_ids,
        owned,
        norm_gain.reshape(1, -1),
        jnp.asarray(cosine),
        jnp.asarray(sine),
        w_query,
        w_key,
        w_value,
        key_cache,
        value_cache,
    )


def solution(mesh):
    in_specs = (
        P(("groups", "particle"), None),
        P(("groups", "particle")),
        P("particle", "head"),
        P(),
        P(None, "head"),
        P(None, "head"),
        P(None, "head"),
        P(("groups", "particle"), "head", None, None),
        P(("groups", "particle"), "head", None, None),
    )
    out_specs = P(("groups", "particle"), None, "head")
    return jax.shard_map(
        functools.partial(per_device, mesh.shape["particle"], mesh.shape["head"]),
        mesh=mesh,
        in_specs=in_specs,
        out_specs=out_specs,
        check_vma=False,
    )
```

```python
import functools
import itertools
import math

import jax
import jax.numpy as jnp
import numpy as np
from jax import lax
from jax.experimental import pallas as pl
from jax.experimental.pallas import tpu as pltpu
from jax.sharding import PartitionSpec as P

MESH = pl.DeviceIdType.MESH
VMEM_LIMIT = 48 * 1024 * 1024


def remote(src, dst, send_sem, recv_sem, **where):
    return pltpu.make_async_remote_copy(
        src_ref=src,
        dst_ref=dst,
        send_sem=send_sem,
        recv_sem=recv_sem,
        device_id=where,
        device_id_type=MESH,
    )


def ids_kernel(groups, n, steps, vocab_rows, widths, cap, hubs, ids_ref, all_ref, plan_ref, send_sem, recv_sem):
    group, me = lax.axis_index("groups"), lax.axis_index("particle")
    peers = [
        (lax.rem(group + g, groups), lax.rem(me + r, n))
        for r in range(n)
        for g in range(groups)
        if r or g
    ]
    barrier = pltpu.get_barrier_semaphore()
    for g, peer in peers:
        pl.semaphore_signal(
            barrier, inc=1, device_id={"groups": g, "particle": peer}, device_id_type=MESH
        )
    pl.semaphore_wait(barrier, len(peers))
    copies = [
        remote(
            ids_ref, all_ref.at[group, me], send_sem.at[i], recv_sem.at[i], groups=g, particle=peer
        )
        for i, (g, peer) in enumerate(peers)
    ]
    for copy in copies:
        copy.start()
    all_ref[group, me] = ids_ref[...]
    for copy in copies:
        copy.wait()
    fallback = len(hubs) ** groups
    if not hubs:
        plan_ref[0] = fallback
        return

    particles, lanes = ids_ref.shape
    lane = lax.broadcasted_iota(jnp.int32, (particles, lanes), 1)
    child = lax.broadcasted_iota(jnp.int32, (particles, lanes), 0)
    plan = jnp.int32(0)
    fits = jnp.bool_(True)
    most = jnp.zeros((particles, lanes), jnp.int32)
    for g in range(groups):
        bad = [jnp.zeros((particles, lanes), jnp.int32) for _ in hubs]
        for c in range(n):
            block = all_ref[g, c]
            for owner in range(n):
                inside = (block >= owner * vocab_rows) & (block < (owner + 1) * vocab_rows)
                inside = (inside & (lane < steps)).astype(jnp.int32)
                amount = jnp.sum(jnp.sum(inside, axis=0, keepdims=True), axis=1, keepdims=True)
                most = jnp.maximum(most, jnp.broadcast_to(amount, most.shape))
            for i, hub in enumerate(hubs):
                good = (block >= c * particles) & (block < (c + 1) * particles)
                for d, width in ((d, w) for r, w in widths.items() for d, w in ((r, w), (-r, w))):
                    p = c + d
                    if (d > 0 and p <= hub) or (d < 0 and p >= hub):
                        within = child >= particles - width if d > 0 else child < width
                        here = (block >= p * particles) & (block < (p + 1) * particles)
                        good = good | (here & within)
                bad[i] = jnp.maximum(bad[i], jnp.where(good | (lane != steps), 0, 1))
        flags = [jnp.max(x) == 0 for x in bad]
        choice, some = jnp.int32(0), jnp.bool_(False)
        for i in reversed(range(len(hubs))):
            choice = jnp.where(flags[i], i, choice)
            some = some | flags[i]
        fits = fits & some
        plan = plan * len(hubs) + choice
    fits = fits & (jnp.max(most) <= cap)
    plan_ref[0] = jnp.where(fits, plan, fallback)


def rows_kernel(n, particles, steps, tile, cap, ids_ref, table_ref, out_ref, hot_ref, blocks, found, hot, listed, counts, sem):
    vocab_rows = table_ref.shape[0]
    group, me = lax.axis_index("groups"), lax.axis_index("particle")
    first = me * vocab_rows
    trash = out_ref.shape[0]

    def look(dest, count):
        def look_child(child, carry):
            count, packed = carry
            for step in range(steps):
                local = ids_ref[group, dest, child, step] - first
                owned = jnp.logical_and(local >= 0, local < vocab_rows)
                spot = child * steps + step if cap is None else packed
                listed[0, count] = dest * (particles * steps if cap is None else cap) + spot
                listed[1, count] = local

                @pl.when(owned)
                def _():
                    start = pl.multiple_of((local // tile) * tile, tile)
                    pltpu.make_async_copy(
                        table_ref.at[pl.ds(start, tile)], blocks.at[count], sem
                    ).start()

                count = count + owned.astype(jnp.int32)
                packed = packed + owned.astype(jnp.int32)
            return count, packed

        return lax.fori_loop(0, particles, look_child, (count, jnp.int32(0)))[0]

    count = lax.fori_loop(0, n, look, jnp.int32(0))
    for extra in range(4):
        listed[0, count + extra] = trash
        listed[1, count + extra] = 0
    found[...] = jnp.zeros_like(found)

    if cap is not None:
        for owner in range(n):
            counts[owner] = 0
        lane = lax.broadcasted_iota(jnp.int32, (1, n * cap), 1)

        def place(child, carry):
            for step in range(steps):
                owner = lax.div(ids_ref[group, me, child, step], jnp.int32(vocab_rows))
                rank = counts[owner]
                counts[owner] = rank + 1
                hot[pl.ds(child * steps + step, 1), :] = jnp.where(
                    lane == owner * cap + rank, 1.0, 0.0
                )
            return carry

        lax.fori_loop(0, particles, place, 0)
        hot_ref[...] = hot[...].astype(hot_ref.dtype)
    else:
        hot_ref[...] = jnp.zeros_like(hot_ref)

    def arrive(slot, carry):
        pltpu.make_async_copy(table_ref.at[pl.ds(0, tile)], blocks.at[slot], sem).wait()
        return carry

    lax.fori_loop(0, count, arrive, 0)

    def pick(some, carry):
        for offset in range(4):
            slot = some * 4 + offset
            row = lax.rem(listed[1, slot], tile)
            block = blocks[slot].astype(jnp.float32)
            here = lax.broadcasted_iota(jnp.int32, block.shape, 0) == row
            found[pl.ds(listed[0, slot], 1), :] = jnp.sum(
                jnp.where(here, block, 0.0), axis=0, keepdims=True
            )
        return carry

    lax.fori_loop(0, (count + 3) // 4, pick, 0)
    out_ref[...] = found[:trash, :].astype(out_ref.dtype)


def main_kernel(
    n,
    heads,
    deltas,
    widths,
    cap,
    hubs,
    ids_ref,
    rows_ref,
    hot_ref,
    gain_ref,
    cos_ref,
    sin_ref,
    wq_hbm,
    wk_hbm,
    wv_hbm,
    kc_hbm,
    vc_hbm,
    out_ref,
    wq,
    wk,
    wv,
    kc,
    vc,
    came,
    emb,
    proj,
    query,
    new_k,
    new_v,
    q_in,
    res_out,
    lse_out,
    res_in,
    lse_in,
    own_res,
    load_sem,
    a_send,
    a_recv,
    x_send,
    x_recv,
    s_send,
    s_recv,
    q_send,
    q_recv,
    r_send,
    r_recv,
    l_send,
    l_recv,
):
    particles, kv = kc.shape[0], kc.shape[1]
    steps = cos_ref.shape[0]
    head_size = kc.shape[3]
    tokens = particles * steps
    local_heads = wq.shape[1] // head_size
    group = local_heads // kv
    rows = group * steps
    depth = rows_ref.shape[1]
    scale = 1.0 / math.sqrt(head_size)
    z = lax.axis_index("particle")
    h = lax.axis_index("head")
    y = lax.axis_index("groups")
    cores = 2
    chips = heads // cores
    chip, core = h // cores, lax.rem(h, cores)
    sibling = chip * cores + 1 - core

    loads = [
        pltpu.make_async_copy(src, dst, load_sem.at[i])
        for i, (src, dst) in enumerate(
            ((wq_hbm, wq), (wk_hbm, wk), (wv_hbm, wv), (kc_hbm, kc), (vc_hbm, vc))
        )
    ]
    for load in loads:
        load.start()

    z_peers = [lax.rem(z + r, n) for r in range(1, n)]
    x_peers = [lax.rem(chip + r, chips) * cores + core for r in range(1, chips)]
    x_from = [lax.rem(chip - r + chips, chips) * cores + core for r in range(1, chips)]
    barrier = pltpu.get_barrier_semaphore()
    for peer in z_peers:
        pl.semaphore_signal(barrier, inc=1, device_id={"particle": peer}, device_id_type=MESH)
    for peer in x_peers + [sibling]:
        pl.semaphore_signal(barrier, inc=1, device_id={"head": peer}, device_id_type=MESH)
    pl.semaphore_wait(barrier, n - 1 + chips)

    chunk = tokens if cap is None else cap

    def of(peer):
        return rows_ref.at[pl.ds(pl.multiple_of(peer * chunk, chunk), chunk)]

    a_copies = [
        remote(of(peer), came.at[z], a_send.at[r], a_recv.at[r], particle=peer)
        for r, peer in enumerate(z_peers)
    ]
    for copy in a_copies:
        copy.start()
    came[z] = of(z)[...]
    for copy in a_copies:
        copy.wait_recv()
    if cap is None:
        total = came[0]
        for owner in range(1, n):
            total = total + came[owner]
        emb[h] = total
    else:
        packed = came[...].reshape(n * cap, depth)
        emb[h] = jnp.dot(hot_ref[...], packed, preferred_element_type=jnp.float32).astype(
            jnp.bfloat16
        )

    sib_own = remote(emb.at[h], emb.at[h], s_send.at[0], s_recv.at[0], head=sibling)
    x_copies = [
        remote(emb.at[h], emb.at[h], x_send.at[r], x_recv.at[r], head=peer)
        for r, peer in enumerate(x_peers)
    ]
    for copy in x_copies:
        copy.start()
    sib_own.start()
    for load in loads[:3]:
        load.wait()

    square = jnp.zeros((tokens, 1), jnp.float32)

    def contract(square, index, first):
        part = emb[index].astype(jnp.float32)
        square = square + jnp.sum(part * part, axis=1, keepdims=True)
        at = pl.ds(pl.multiple_of(index * depth, depth), depth)
        scaled = (part * gain_ref[:, at].astype(jnp.float32)).astype(jnp.bfloat16)
        column = 0
        for weight in (wq, wk, wv):
            for begin in range(0, weight.shape[1], 128 if weight.shape[1] % 256 else 256):
                width = 128 if weight.shape[1] % 256 else 256
                product = jnp.dot(
                    scaled,
                    weight[at, begin : begin + width],
                    preferred_element_type=jnp.float32,
                )
                where = slice(column, column + width)
                if first:
                    proj[:, where] = product
                else:
                    proj[:, where] += product
                column += width
        return square

    square = contract(square, h, True)
    sib_own.wait_recv()
    square = contract(square, sibling, False)
    forwards = []
    for r, (copy, source) in enumerate(zip(x_copies, x_from)):
        copy.wait_recv()
        forward = remote(
            emb.at[source], emb.at[source], s_send.at[r + 1], s_recv.at[r + 1], head=sibling
        )
        forward.start()
        forwards.append(forward)
        square = contract(square, source, False)
    for r, forward in enumerate(forwards):
        forward.wait_recv()
        source = lax.rem(chip - (r + 1) + chips, chips) * cores + 1 - core
        square = contract(square, source, False)

    norm = lax.rsqrt(square * (1.0 / (depth * heads)) + 1e-5)
    cosine, sine = cos_ref[...], sin_ref[...]

    def spin(column):
        value = proj[:, column * head_size : (column + 1) * head_size] * norm
        turned = pltpu.roll(value, head_size // 2, 1)
        shape = (particles, steps, head_size)
        return value.reshape(shape) * cosine[None] + turned.reshape(shape) * sine[None]

    for k in range(kv):
        for pair in range(0, group, 2):
            both = jnp.concatenate([spin(k * group + pair), spin(k * group + pair + 1)], axis=1)
            query[:, k, pair * steps : (pair + 2) * steps, :] = both.astype(jnp.bfloat16)

    def span(d):
        width = widths[abs(d)]
        return (0 if d < 0 else particles - width), width

    def reaches(d, at=z):
        if hubs is None:
            return jnp.logical_and(at + d >= 0, at + d < n)
        hub = jnp.int32(hubs[-1])
        for g in range(len(hubs) - 1):
            hub = jnp.where(y == g, hubs[g], hub)
        if d > 0:
            return at + d <= hub
        return at + d >= hub

    def hears(d):
        known = jnp.logical_and(z - d >= 0, z - d < n)
        return jnp.logical_and(known, reaches(d, z - d))

    def query_copy(i, d):
        begin, width = span(d)
        return remote(
            query.at[pl.ds(begin, width)],
            q_in.at[i, pl.ds(begin, width)],
            q_send.at[i],
            q_recv.at[i],
            particle=z + d,
        )

    def back_copies(i, d):
        begin, width = span(d)
        return (
            remote(
                res_out.at[i, pl.ds(begin, width)],
                res_in.at[i, pl.ds(begin, width)],
                r_send.at[i],
                r_recv.at[i],
                particle=z - d,
            ),
            remote(
                lse_out.at[i], lse_in.at[i], l_send.at[i], l_recv.at[i], particle=z - d
            ),
        )

    for i, d in enumerate(deltas):

        @pl.when(reaches(d))
        def _():
            query_copy(i, d).start()

    for k in range(kv):
        new_k[k] = spin(local_heads + k).reshape(tokens, head_size).astype(jnp.bfloat16)
        base = (local_heads + kv + k) * head_size
        new_v[k] = (proj[:, base : base + head_size] * norm).astype(jnp.bfloat16)

    own_lse = []
    for k in range(kv):
        q_rows = query[:, k].reshape(particles * rows, head_size)
        scores = lax.dot_general(
            q_rows, new_k[k], (((1,), (1,)), ((), ())), preferred_element_type=jnp.float32
        ) * scale
        at_row = lax.broadcasted_iota(jnp.int32, scores.shape, 0)
        at_key = lax.broadcasted_iota(jnp.int32, scores.shape, 1)
        seen = jnp.logical_and(
            at_row // rows == at_key // steps,
            lax.rem(at_key, steps) <= lax.rem(at_row, steps),
        )
        scores = jnp.where(seen, scores, -1e30)
        top = jnp.max(scores, axis=1, keepdims=True)
        weight = jnp.exp(scores - top)
        weight = jnp.where(seen, weight, 0.0)
        amount = jnp.sum(weight, axis=1, keepdims=True)
        summed = jnp.dot(weight.astype(jnp.bfloat16), new_v[k], preferred_element_type=jnp.float32)
        own_res[k] = summed / amount
        own_lse.append(top + jnp.log(amount))

    for load in loads[3:]:
        load.wait()

    lane = lax.broadcasted_iota(jnp.int32, (rows, 128), 1)

    def attend(i, source_query, begin, width, source):
        some = 4 if width % 4 == 0 else 1

        def some_children(block, lse):
            for offset in range(some):
                child = begin + block * some + offset
                parent = ids_ref[y, source, child, steps] - z * particles
                parent = jnp.minimum(jnp.maximum(parent, 0), particles - 1)
                for k in range(kv):
                    scores = lax.dot_general(
                        source_query(child, k),
                        kc[parent, k],
                        (((1,), (1,)), ((), ())),
                        preferred_element_type=jnp.float32,
                    ) * scale
                    top = jnp.max(scores, axis=1, keepdims=True)
                    weight = jnp.exp(scores - top)
                    amount = jnp.sum(weight, axis=1, keepdims=True)
                    summed = jnp.dot(
                        weight.astype(jnp.bfloat16),
                        vc[parent, k],
                        preferred_element_type=jnp.float32,
                    )
                    res_out[i, child, k] = (summed / amount).astype(jnp.bfloat16)
                    lse = jnp.where(lane == child * kv + k, top + jnp.log(amount), lse)
            return lse

        lse_out[i] = lax.fori_loop(
            0, width // some, some_children, jnp.zeros((rows, 128), jnp.float32)
        )

    own = len(deltas)
    attend(own, lambda child, k: query[child, k], 0, particles, z)
    res_in[own] = res_out[own]
    lse_in[own] = lse_out[own]

    for i, d in enumerate(deltas):

        @pl.when(hears(d))
        def _():
            query_copy(i, d).wait_recv()
            begin, width = span(d)
            attend(i, lambda child, k: q_in[i, child, k], begin, width, z - d)
            for copy in back_copies(i, d):
                copy.start()

    for i, d in enumerate(deltas):

        @pl.when(reaches(d))
        def _():
            for copy in back_copies(i, d):
                copy.wait_recv()

    for child in range(particles):
        owner = ids_ref[y, z, child, steps] // particles
        slot = jnp.int32(own)
        for i, d in enumerate(deltas):
            slot = jnp.where(owner - z == d, i, slot)
        parts = []
        lse_tile = lse_in[slot]
        for k in range(kv):
            cached = res_in[slot, child, k].astype(jnp.float32)
            cached_lse = jnp.sum(
                jnp.where(lane == child * kv + k, lse_tile, 0.0), axis=1, keepdims=True
            )
            at = slice(child * rows, (child + 1) * rows)
            mine, mine_lse = own_res[k, at, :], own_lse[k][at, :]
            top = jnp.maximum(cached_lse, mine_lse)
            cached_factor = jnp.exp(cached_lse - top)
            mine_factor = jnp.exp(mine_lse - top)
            mixed = (cached * cached_factor + mine * mine_factor) / (cached_factor + mine_factor)
            for g in range(group):
                parts.append(mixed[g * steps : (g + 1) * steps, :])
        out_ref[child] = jnp.concatenate(parts, axis=1).astype(out_ref.dtype)

    for copy in a_copies + x_copies + forwards + [sib_own]:
        copy.wait_send()
    for i, d in enumerate(deltas):

        @pl.when(reaches(d))
        def _():
            query_copy(i, d).wait_send()

        @pl.when(hears(d))
        def _():
            for copy in back_copies(i, d):
                copy.wait_send()


def tables(steps, head_size, first_position):
    half = head_size // 2
    freqs = 500000.0 ** (-(2.0 * np.arange(half)) / head_size)
    phase = (first_position + np.arange(steps))[:, None] * freqs[None, :]
    cosine, sine = np.cos(phase), np.sin(phase)
    return (
        np.concatenate([cosine, cosine], axis=1).astype(np.float32),
        np.concatenate([-sine, sine], axis=1).astype(np.float32),
    )


def per_device(
    groups,
    n,
    heads,
    tokens,
    ancestors,
    embedding,
    norm_gain,
    w_query,
    w_key,
    w_value,
    key_cache,
    value_cache,
):
    particles, steps = tokens.shape
    _, kv, context, head_size = key_cache.shape
    local_heads = w_query.shape[1] // head_size
    vocab_rows, depth = embedding.shape
    count = particles * steps
    rows = local_heads // kv * steps
    vmem = pl.BlockSpec(memory_space=pltpu.VMEM)
    smem = pl.BlockSpec(memory_space=pltpu.SMEM)
    hbm = pl.BlockSpec(memory_space=pl.ANY)
    dma = pltpu.SemaphoreType.DMA

    ids = jnp.concatenate([tokens, ancestors[:, None]], axis=1)
    ids = jnp.pad(ids, ((0, 0), (0, 128 - ids.shape[1])))
    cap = count // 2
    narrow = {1: particles, 2: particles // 2}
    hubs = tuple(range(1, n - 1)) if n <= 4 else ()
    peers = groups * n - 1
    all_ids, plan = pl.pallas_call(
        functools.partial(ids_kernel, groups, n, steps, vocab_rows, narrow, cap, hubs),
        out_shape=(
            jax.ShapeDtypeStruct((groups, n, particles, 128), jnp.int32),
            jax.ShapeDtypeStruct((1,), jnp.int32),
        ),
        in_specs=[vmem],
        out_specs=(vmem, smem),
        scratch_shapes=[dma((peers,)), dma((peers,))],
        compiler_params=pltpu.CompilerParams(collective_id=0, has_side_effects=True),
    )(ids)

    tile = 16 if vocab_rows % 16 == 0 else 8
    chips = heads // 2
    cosine, sine = tables(steps, head_size, context)
    bf16, f32, i32 = jnp.bfloat16, jnp.float32, jnp.int32

    def run(widths, cap, hubs, number):
        chunk = count if cap is None else cap
        deltas = [d for r in widths for d in (r, -r)]
        slots = len(deltas)
        owned, hot = pl.pallas_call(
            functools.partial(rows_kernel, n, particles, steps, tile, cap),
            out_shape=(
                jax.ShapeDtypeStruct((n * chunk, depth), bf16),
                jax.ShapeDtypeStruct((count, n * chunk), bf16),
            ),
            in_specs=[smem, hbm],
            out_specs=(vmem, vmem),
            scratch_shapes=[
                pltpu.VMEM((n * count + 4, tile, depth), bf16),
                pltpu.VMEM((n * chunk + 8, depth), f32),
                pltpu.VMEM((count, n * chunk), f32),
                pltpu.SMEM((2, n * count + 4), i32),
                pltpu.SMEM((n,), i32),
                dma,
            ],
            compiler_params=pltpu.CompilerParams(vmem_limit_bytes=VMEM_LIMIT),
        )(all_ids, embedding)

        return pl.pallas_call(
            functools.partial(main_kernel, n, heads, deltas, widths, cap, hubs),
            out_shape=jax.ShapeDtypeStruct((particles, steps, local_heads * head_size), bf16),
            in_specs=[smem] + [vmem] * 5 + [hbm] * 5,
            out_specs=vmem,
            scratch_shapes=[
                pltpu.VMEM(w_query.shape, bf16),
                pltpu.VMEM(w_key.shape, bf16),
                pltpu.VMEM(w_value.shape, bf16),
                pltpu.VMEM(key_cache.shape, bf16),
                pltpu.VMEM(value_cache.shape, bf16),
                pltpu.VMEM((n, chunk, depth), bf16),
                pltpu.VMEM((heads, count, depth), bf16),
                pltpu.VMEM((count, (local_heads + 2 * kv) * head_size), f32),
                pltpu.VMEM((particles, kv, rows, head_size), bf16),
                pltpu.VMEM((kv, count, head_size), bf16),
                pltpu.VMEM((kv, count, head_size), bf16),
                pltpu.VMEM((slots, particles, kv, rows, head_size), bf16),
                pltpu.VMEM((slots + 1, particles, kv, rows, head_size), bf16),
                pltpu.VMEM((slots + 1, rows, 128), f32),
                pltpu.VMEM((slots + 1, particles, kv, rows, head_size), bf16),
                pltpu.VMEM((slots + 1, rows, 128), f32),
                pltpu.VMEM((kv, particles * rows, head_size), f32),
                dma((5,)),
                dma((n - 1,)),
                dma((n - 1,)),
                dma((max(chips - 1, 1),)),
                dma((max(chips - 1, 1),)),
                dma((chips,)),
                dma((chips,)),
            ]
            + [dma((slots,))] * 6,
            compiler_params=pltpu.CompilerParams(
                collective_id=1 + number, has_side_effects=True, vmem_limit_bytes=VMEM_LIMIT
            ),
        )(
            all_ids,
            owned,
            hot,
            norm_gain.reshape(1, -1),
            jnp.asarray(cosine),
            jnp.asarray(sine),
            w_query,
            w_key,
            w_value,
            key_cache,
            value_cache,
        )

    chosen = list(itertools.product(hubs, repeat=groups)) if hubs else []
    branches = [
        functools.partial(run, narrow, cap, pair, number) for number, pair in enumerate(chosen)
    ]
    full = {r: particles for r in range(1, n)}
    branches.append(functools.partial(run, full, None, None, len(chosen)))
    if not chosen:
        return branches[0]()
    return lax.switch(plan[0], branches)


def solution(mesh):
    in_specs = (
        P(("groups", "particle"), None),
        P(("groups", "particle")),
        P("particle", "head"),
        P(),
        P(None, "head"),
        P(None, "head"),
        P(None, "head"),
        P(("groups", "particle"), "head", None, None),
        P(("groups", "particle"), "head", None, None),
    )
    out_specs = P(("groups", "particle"), None, "head")
    return jax.shard_map(
        functools.partial(
            per_device, mesh.shape["groups"], mesh.shape["particle"], mesh.shape["head"]
        ),
        mesh=mesh,
        in_specs=in_specs,
        out_specs=out_specs,
        check_vma=False,
    )
```

```python
import functools
import itertools
import math

import jax
import jax.numpy as jnp
import numpy as np
from jax import lax
from jax.experimental import pallas as pl
from jax.experimental.pallas import tpu as pltpu
from jax.sharding import PartitionSpec as P

MESH = pl.DeviceIdType.MESH
VMEM_LIMIT = 48 * 1024 * 1024


def remote(src, dst, send_sem, recv_sem, **where):
    return pltpu.make_async_remote_copy(
        src_ref=src,
        dst_ref=dst,
        send_sem=send_sem,
        recv_sem=recv_sem,
        device_id=where,
        device_id_type=MESH,
    )


def ids_kernel(groups, n, steps, vocab_rows, widths, cap, hubs, tokens_ref, parents_ref, all_ref, plan_ref, ids_ref, send_sem, recv_sem):
    group, me = lax.axis_index("groups"), lax.axis_index("particle")
    peers = [
        (lax.rem(group + g, groups), lax.rem(me + r, n))
        for r in range(n)
        for g in range(groups)
        if r or g
    ]
    barrier = pltpu.get_barrier_semaphore()
    for g, peer in peers:
        pl.semaphore_signal(
            barrier, inc=1, device_id={"groups": g, "particle": peer}, device_id_type=MESH
        )
    particles, lanes = ids_ref.shape
    lane = lax.broadcasted_iota(jnp.int32, (particles, lanes), 1)
    child = lax.broadcasted_iota(jnp.int32, (particles, lanes), 0)
    ids = jnp.zeros((particles, lanes), jnp.int32)
    for i in range(particles):
        ids = jnp.where(child == i, parents_ref[i], ids)
    ids_ref[...] = ids
    ids_ref[:, :steps] = tokens_ref[...]
    pl.semaphore_wait(barrier, len(peers))
    copies = [
        remote(
            ids_ref, all_ref.at[group, me], send_sem.at[i], recv_sem.at[i], groups=g, particle=peer
        )
        for i, (g, peer) in enumerate(peers)
    ]
    for copy in copies:
        copy.start()
    all_ref[group, me] = ids_ref[...]
    for copy in copies:
        copy.wait()
    fallback = len(hubs) ** groups
    if not hubs:
        plan_ref[0] = fallback
        return

    plan = jnp.int32(0)
    fits = jnp.bool_(True)
    most = jnp.zeros((particles, lanes), jnp.int32)
    for g in range(groups):
        bad = [jnp.zeros((particles, lanes), jnp.int32) for _ in hubs]
        for c in range(n):
            block = all_ref[g, c]
            mark = jnp.where(block >= vocab_rows, 256, 1)
            for owner in range(2, n):
                mark = jnp.where(block >= owner * vocab_rows, 256**owner, mark)
            mark = jnp.where(lane < steps, mark, 0)
            amount = jnp.sum(jnp.sum(mark, axis=0, keepdims=True), axis=1, keepdims=True)
            for owner in range(n):
                most = jnp.maximum(most, jnp.broadcast_to((amount >> (8 * owner)) & 255, most.shape))
            for i, hub in enumerate(hubs):
                good = (block >= c * particles) & (block < (c + 1) * particles)
                for d, width in ((d, w) for r, w in widths.items() for d, w in ((r, w), (-r, w))):
                    p = c + d
                    if (d > 0 and p <= hub) or (d < 0 and p >= hub):
                        within = child >= particles - width if d > 0 else child < width
                        here = (block >= p * particles) & (block < (p + 1) * particles)
                        good = good | (here & within)
                bad[i] = jnp.maximum(bad[i], jnp.where(good | (lane != steps), 0, 1))
        flags = [jnp.max(x) == 0 for x in bad]
        choice, some = jnp.int32(0), jnp.bool_(False)
        for i in reversed(range(len(hubs))):
            choice = jnp.where(flags[i], i, choice)
            some = some | flags[i]
        fits = fits & some
        plan = plan * len(hubs) + choice
    fits = fits & (jnp.max(most) <= cap)
    plan_ref[0] = jnp.where(fits, plan, fallback)


def rows_kernel(n, particles, steps, tile, cap, ids_ref, table_ref, out_ref, hot_ref, blocks, found, hot, listed, sem):
    vocab_rows = table_ref.shape[0]
    group, me = lax.axis_index("groups"), lax.axis_index("particle")
    first = me * vocab_rows
    trash = out_ref.shape[0]

    def look(dest, count):
        def look_child(child, carry):
            count, packed = carry
            for step in range(steps):
                local = ids_ref[group, dest, child, step] - first
                owned = jnp.logical_and(local >= 0, local < vocab_rows)
                spot = child * steps + step if cap is None else packed
                listed[0, count] = dest * (particles * steps if cap is None else cap) + spot
                listed[1, count] = local

                @pl.when(owned)
                def _():
                    start = pl.multiple_of(local - (local & (tile - 1)), tile)
                    pltpu.make_async_copy(
                        table_ref.at[pl.ds(start, tile)], blocks.at[count], sem
                    ).start()

                count = count + owned.astype(jnp.int32)
                packed = packed + owned.astype(jnp.int32)
            return count, packed

        return lax.fori_loop(0, particles, look_child, (count, jnp.int32(0)))[0]

    count = lax.fori_loop(0, n, look, jnp.int32(0))
    for extra in range(4):
        listed[0, count + extra] = trash
        listed[1, count + extra] = 0
    found[...] = jnp.zeros_like(found)

    if cap is not None:
        lane = lax.broadcasted_iota(jnp.int32, (1, n * cap), 1)

        def place(child, counts):
            for step in range(steps):
                token = ids_ref[group, me, child, step]
                owner = jnp.int32(0)
                for other in range(1, n):
                    owner = owner + (token >= other * vocab_rows).astype(jnp.int32)
                rank = (counts >> (8 * owner)) & 255
                counts = counts + (jnp.int32(1) << (8 * owner))
                hot[pl.ds(child * steps + step, 1), :] = jnp.where(
                    lane == owner * cap + rank, 1.0, 0.0
                )
            return counts

        lax.fori_loop(0, particles, place, jnp.int32(0))
        hot_ref[...] = hot[...].astype(hot_ref.dtype)
    else:
        hot_ref[...] = jnp.zeros_like(hot_ref)

    def arrive(slot, carry):
        pltpu.make_async_copy(table_ref.at[pl.ds(0, tile)], blocks.at[slot], sem).wait()
        return carry

    lax.fori_loop(0, count, arrive, 0)

    def pick(some, carry):
        for offset in range(4):
            slot = some * 4 + offset
            row = listed[1, slot] & (tile - 1)
            block = blocks[slot].astype(jnp.float32)
            here = lax.broadcasted_iota(jnp.int32, block.shape, 0) == row
            found[pl.ds(listed[0, slot], 1), :] = jnp.sum(
                jnp.where(here, block, 0.0), axis=0, keepdims=True
            )
        return carry

    lax.fori_loop(0, (count + 3) // 4, pick, 0)
    out_ref[...] = found[:trash, :].astype(out_ref.dtype)


def main_kernel(
    n,
    heads,
    deltas,
    widths,
    cap,
    hubs,
    ids_ref,
    rows_ref,
    hot_ref,
    gain_in,
    bias_ref,
    cos_ref,
    sin_ref,
    wq,
    wk,
    wv,
    kc,
    vc,
    out_ref,
    came,
    emb,
    proj,
    query,
    new_k,
    new_v,
    q_in,
    res_out,
    lse_out,
    res_in,
    lse_in,
    own_res,
    gain_ref,
    a_send,
    a_recv,
    x_send,
    x_recv,
    s_send,
    s_recv,
    q_send,
    q_recv,
    r_send,
    r_recv,
    l_send,
    l_recv,
):
    particles, kv = kc.shape[0], kc.shape[1]
    steps = cos_ref.shape[0]
    head_size = kc.shape[3]
    half = particles // 2
    tokens = particles * steps
    local_heads = wq.shape[1] // head_size
    group = local_heads // kv
    rows = group * steps
    depth = rows_ref.shape[1]
    scale = 1.0 / math.sqrt(head_size)
    z = lax.axis_index("particle")
    h = lax.axis_index("head")
    y = lax.axis_index("groups")
    cores = 2
    chips = heads // cores
    chip, core = h // cores, lax.rem(h, cores)
    sibling = chip * cores + 1 - core

    z_peers = [lax.rem(z + r, n) for r in range(1, n)]
    x_peers = [lax.rem(chip + r, chips) * cores + core for r in range(1, chips)]
    x_from = [lax.rem(chip - r + chips, chips) * cores + core for r in range(1, chips)]
    barrier = pltpu.get_barrier_semaphore()
    for peer in z_peers:
        pl.semaphore_signal(barrier, inc=1, device_id={"particle": peer}, device_id_type=MESH)
    for peer in x_peers + [sibling]:
        pl.semaphore_signal(barrier, inc=1, device_id={"head": peer}, device_id_type=MESH)
    pl.semaphore_wait(barrier, n - 1 + chips)

    chunk = tokens if cap is None else cap

    def of(peer):
        return rows_ref.at[pl.ds(pl.multiple_of(peer * chunk, chunk), chunk)]

    cut = depth // 2
    a_copies = [
        [
            remote(
                rows_ref.at[
                    pl.ds(pl.multiple_of(peer * chunk, chunk), chunk), pl.ds(part * cut, cut)
                ],
                came.at[part, z],
                a_send.at[part, r],
                a_recv.at[part, r],
                particle=peer,
            )
            for r, peer in enumerate(z_peers)
        ]
        for part in range(2)
    ]
    for copy in a_copies[0]:
        copy.start()
    own_rows = of(z)[...]
    for part in range(2):
        came[part, z] = own_rows[:, part * cut : (part + 1) * cut]
    gain_ref[...] = gain_in[...].astype(jnp.float32).reshape(gain_ref.shape)
    for copy in a_copies[0]:
        copy.wait_send()
    for copy in a_copies[1]:
        copy.start()

    def share(part, source, sends, receives, slot, peer):
        block = emb.at[part, source]
        return remote(block, block, sends.at[part, slot], receives.at[part, slot], head=peer)

    x_copies = [
        [share(part, h, x_send, x_recv, r, peer) for r, peer in enumerate(x_peers)]
        for part in range(2)
    ]
    sib_copies = [share(part, h, s_send, s_recv, 0, sibling) for part in range(2)]
    forwards = [
        [share(part, source, s_send, s_recv, r + 1, sibling) for r, source in enumerate(x_from)]
        for part in range(2)
    ]

    def contract(square, index, part, first=False):
        values = emb[part, index].astype(jnp.float32)
        square = square + jnp.sum(values * values, axis=1, keepdims=True)
        at = pl.ds(pl.multiple_of(index * depth + part * cut, cut), cut)
        scaled = (values * gain_ref[:, at]).astype(jnp.bfloat16)
        column = 0
        for weight in (wq, wk, wv):
            width = 128 if weight.shape[1] % 256 else 256
            for begin in range(0, weight.shape[1], width):
                product = jnp.dot(
                    scaled,
                    weight[at, begin : begin + width],
                    preferred_element_type=jnp.float32,
                )
                where = slice(column, column + width)
                if first:
                    proj[:, where] = product
                else:
                    proj[:, where] += product
                column += width
        return square

    square = jnp.zeros((tokens, 1), jnp.float32)
    for part in range(2):
        for copy in a_copies[part]:
            copy.wait_recv()
        if cap is None:
            total = came[part, 0]
            for owner in range(1, n):
                total = total + came[part, owner]
            emb[part, h] = total
        else:
            packed = came[part].reshape(n * cap, cut)
            emb[part, h] = jnp.dot(
                hot_ref[...], packed, preferred_element_type=jnp.float32
            ).astype(jnp.bfloat16)
        for copy in x_copies[part]:
            copy.start()
        sib_copies[part].start()
        square = contract(square, h, part, part == 0)
    for part in range(2):
        sib_copies[part].wait_recv()
        square = contract(square, sibling, part)
        for copy, forward in zip(x_copies[part], forwards[part]):
            copy.wait_recv()
            forward.start()
    for part in range(2):
        for source in x_from:
            square = contract(square, source, part)
    for part in range(2):
        for r, forward in enumerate(forwards[part]):
            forward.wait_recv()
            source = lax.rem(chip - (r + 1) + chips, chips) * cores + 1 - core
            square = contract(square, source, part)

    norm = lax.rsqrt(square * (1.0 / (depth * heads)) + 1e-5)
    cosine, sine = cos_ref[...], sin_ref[...]

    def spin(column):
        value = proj[:, column * head_size : (column + 1) * head_size] * norm
        turned = pltpu.roll(value, head_size // 2, 1)
        shape = (particles, steps, head_size)
        return value.reshape(shape) * cosine[None] + turned.reshape(shape) * sine[None]

    for k in range(kv):
        for pair in range(0, group, 2):
            both = jnp.concatenate([spin(k * group + pair), spin(k * group + pair + 1)], axis=1)
            query[:, k, pair * steps : (pair + 2) * steps, :] = both.astype(jnp.bfloat16)

    def span(d):
        width = widths[abs(d)]
        return (0 if d < 0 else particles - width), width

    hub = None
    if hubs is not None:
        hub = jnp.int32(hubs[-1])
        for g in range(len(hubs) - 1):
            hub = jnp.where(y == g, hubs[g], hub)

    def reaches(d):
        if hub is None:
            return jnp.logical_and(z + d >= 0, z + d < n)
        return z + d <= hub if d > 0 else z + d >= hub

    def hears(d):
        known = jnp.logical_and(z - d >= 0, z - d < n)
        if hub is None:
            return known
        return jnp.logical_and(known, jnp.where(d > 0, z <= hub, z >= hub))

    def pieces(d):
        begin, width = span(d)
        return range(begin // half, (begin + width) // half)

    work = sorted(
        ((i, d, piece, order) for i, d in enumerate(deltas) for order, piece in enumerate(pieces(d))),
        key=lambda item: item[3],
    )

    def query_copy(i, d, piece):
        return remote(
            query.at[pl.ds(piece * half, half)],
            q_in.at[i, pl.ds(piece * half, half)],
            q_send.at[i, piece],
            q_recv.at[i, piece],
            particle=z + d,
        )

    def back_copies(i, d, piece):
        return (
            remote(
                res_out.at[i, pl.ds(piece * half, half)],
                res_in.at[i, pl.ds(piece * half, half)],
                r_send.at[i, piece],
                r_recv.at[i, piece],
                particle=z - d,
            ),
            remote(
                lse_out.at[i, piece],
                lse_in.at[i, piece],
                l_send.at[i, piece],
                l_recv.at[i, piece],
                particle=z - d,
            ),
        )

    for i, d, piece, _ in work:

        @pl.when(reaches(d))
        def _():
            query_copy(i, d, piece).start()

    for k in range(kv):
        new_k[k] = spin(local_heads + k).reshape(tokens, head_size).astype(jnp.bfloat16)
        base = (local_heads + kv + k) * head_size
        new_v[k] = (proj[:, base : base + head_size] * norm).astype(jnp.bfloat16)

    own_lse = []
    for k in range(kv):
        q_rows = query[:, k].reshape(particles * rows, head_size)
        scores = lax.dot_general(
            q_rows, new_k[k], (((1,), (1,)), ((), ())), preferred_element_type=jnp.float32
        ) * scale
        scores = scores + bias_ref[...]
        top = jnp.max(scores, axis=1, keepdims=True)
        weight = jnp.exp(scores - top)
        amount = jnp.sum(weight, axis=1, keepdims=True)
        summed = jnp.dot(weight.astype(jnp.bfloat16), new_v[k], preferred_element_type=jnp.float32)
        own_res[k] = summed / amount
        own_lse.append(top + jnp.log(amount))

    lane = lax.broadcasted_iota(jnp.int32, (rows, 128), 1)

    def attend(i, piece, source):
        lse = jnp.zeros((rows, 128), jnp.float32)
        for offset in range(half):
            child = piece * half + offset
            parent = ids_ref[y, source, child, steps] - z * particles
            parent = jnp.minimum(jnp.maximum(parent, 0), particles - 1)
            for k in range(kv):
                scores = lax.dot_general(
                    q_in[i, child, k],
                    kc[parent, k],
                    (((1,), (1,)), ((), ())),
                    preferred_element_type=jnp.float32,
                ) * scale
                top = jnp.max(scores, axis=1, keepdims=True)
                weight = jnp.exp(scores - top)
                amount = jnp.sum(weight, axis=1, keepdims=True)
                summed = jnp.dot(
                    weight.astype(jnp.bfloat16), vc[parent, k], preferred_element_type=jnp.float32
                )
                res_out[i, child, k] = (summed / amount).astype(jnp.bfloat16)
                lse = jnp.where(lane == child * kv + k, top + jnp.log(amount), lse)
        lse_out[i, piece] = lse

    own = len(deltas)
    q_in[own] = query[...]
    todo = [(own, 0, 0), (own, 0, 1)] + [item[:3] for item in work]

    def step_through(t, carry):
        i, d, piece = (jnp.int32(x) for x in todo[-1])
        for number, item in enumerate(todo[:-1]):
            i, d, piece = (jnp.where(t == number, x, v) for x, v in zip(item, (i, d, piece)))
        away = t >= 2
        heard = jnp.logical_and(away, hears(d))

        @pl.when(heard)
        def _():
            query_copy(i, d, piece).wait_recv()

        @pl.when(jnp.logical_or(heard, jnp.logical_not(away)))
        def _():
            attend(i, piece, z - d)

        @pl.when(heard)
        def _():
            for copy in back_copies(i, d, piece):
                copy.start()

        return carry

    lax.fori_loop(0, len(todo), step_through, 0)
    res_in[own] = res_out[own]
    lse_in[own] = lse_out[own]

    for i, d, piece, _ in work:

        @pl.when(reaches(d))
        def _():
            for copy in back_copies(i, d, piece):
                copy.wait_recv()

    for child in range(particles):
        ahead = ids_ref[y, z, child, steps] - z * particles
        slot = jnp.int32(own)
        for i, d in enumerate(deltas):
            there = jnp.logical_and(ahead >= d * particles, ahead < (d + 1) * particles)
            slot = jnp.where(there, i, slot)
        parts = []
        lse_tile = lse_in[slot, child // half]
        for k in range(kv):
            cached = res_in[slot, child, k].astype(jnp.float32)
            cached_lse = jnp.sum(
                jnp.where(lane == child * kv + k, lse_tile, 0.0), axis=1, keepdims=True
            )
            at = slice(child * rows, (child + 1) * rows)
            mine, mine_lse = own_res[k, at, :], own_lse[k][at, :]
            top = jnp.maximum(cached_lse, mine_lse)
            cached_factor = jnp.exp(cached_lse - top)
            mine_factor = jnp.exp(mine_lse - top)
            mixed = (cached * cached_factor + mine * mine_factor) / (cached_factor + mine_factor)
            for g in range(group):
                parts.append(mixed[g * steps : (g + 1) * steps, :])
        out_ref[child] = jnp.concatenate(parts, axis=1).astype(out_ref.dtype)

    for part in range(2):
        for copy in a_copies[1] * part + x_copies[part] + forwards[part] + [sib_copies[part]]:
            copy.wait_send()
    for i, d, piece, _ in work:

        @pl.when(reaches(d))
        def _():
            query_copy(i, d, piece).wait_send()

        @pl.when(hears(d))
        def _():
            for copy in back_copies(i, d, piece):
                copy.wait_send()


def tables(steps, head_size, first_position):
    half = head_size // 2
    freqs = 500000.0 ** (-(2.0 * np.arange(half)) / head_size)
    phase = (first_position + np.arange(steps))[:, None] * freqs[None, :]
    cosine, sine = np.cos(phase), np.sin(phase)
    return (
        np.concatenate([cosine, cosine], axis=1).astype(np.float32),
        np.concatenate([-sine, sine], axis=1).astype(np.float32),
    )


def own_bias(particles, steps, rows):
    at_row = np.arange(particles * rows)[:, None]
    at_key = np.arange(particles * steps)[None, :]
    seen = (at_row // rows == at_key // steps) & (at_key % steps <= at_row % steps)
    return np.where(seen, 0.0, -1e30).astype(np.float32)


def per_device(
    groups,
    n,
    heads,
    tokens,
    ancestors,
    embedding,
    norm_gain,
    w_query,
    w_key,
    w_value,
    key_cache,
    value_cache,
):
    particles, steps = tokens.shape
    _, kv, context, head_size = key_cache.shape
    local_heads = w_query.shape[1] // head_size
    vocab_rows, depth = embedding.shape
    count = particles * steps
    rows = local_heads // kv * steps
    vmem = pl.BlockSpec(memory_space=pltpu.VMEM)
    smem = pl.BlockSpec(memory_space=pltpu.SMEM)
    hbm = pl.BlockSpec(memory_space=pl.ANY)
    dma = pltpu.SemaphoreType.DMA

    cap = count // 2
    narrow = {1: particles, 2: particles // 2}
    hubs = tuple(range(1, n - 1)) if n <= 4 else ()
    peers = groups * n - 1
    all_ids, plan = pl.pallas_call(
        functools.partial(ids_kernel, groups, n, steps, vocab_rows, narrow, cap, hubs),
        out_shape=(
            jax.ShapeDtypeStruct((groups, n, particles, 128), jnp.int32),
            jax.ShapeDtypeStruct((1,), jnp.int32),
        ),
        in_specs=[vmem, smem],
        out_specs=(vmem, smem),
        scratch_shapes=[pltpu.VMEM((particles, 128), jnp.int32), dma((peers,)), dma((peers,))],
        compiler_params=pltpu.CompilerParams(collective_id=0, has_side_effects=True),
    )(tokens, ancestors)

    tile = 16 if vocab_rows % 16 == 0 else 8
    chips = heads // 2
    cosine, sine = tables(steps, head_size, context)
    bf16, f32, i32 = jnp.bfloat16, jnp.float32, jnp.int32

    def run(widths, cap, hubs, number):
        chunk = count if cap is None else cap
        deltas = [d for r in widths for d in (r, -r)]
        slots = len(deltas)
        owned, hot = pl.pallas_call(
            functools.partial(rows_kernel, n, particles, steps, tile, cap),
            out_shape=(
                jax.ShapeDtypeStruct((n * chunk, depth), bf16),
                jax.ShapeDtypeStruct((count, n * chunk), bf16),
            ),
            in_specs=[smem, hbm],
            out_specs=(vmem, vmem),
            scratch_shapes=[
                pltpu.VMEM((n * count + 4, tile, depth), bf16),
                pltpu.VMEM((n * chunk + 8, depth), f32),
                pltpu.VMEM((count, n * chunk), f32),
                pltpu.SMEM((2, n * count + 4), i32),
                dma,
            ],
            compiler_params=pltpu.CompilerParams(vmem_limit_bytes=VMEM_LIMIT),
        )(all_ids, embedding)

        return pl.pallas_call(
            functools.partial(main_kernel, n, heads, deltas, widths, cap, hubs),
            out_shape=jax.ShapeDtypeStruct((particles, steps, local_heads * head_size), bf16),
            in_specs=[smem] + [vmem] * 11,
            out_specs=vmem,
            scratch_shapes=[
                pltpu.VMEM((2, n, chunk, depth // 2), bf16),
                pltpu.VMEM((2, heads, count, depth // 2), bf16),
                pltpu.VMEM((count, (local_heads + 2 * kv) * head_size), f32),
                pltpu.VMEM((particles, kv, rows, head_size), bf16),
                pltpu.VMEM((kv, count, head_size), bf16),
                pltpu.VMEM((kv, count, head_size), bf16),
                pltpu.VMEM((slots + 1, particles, kv, rows, head_size), bf16),
                pltpu.VMEM((slots + 1, particles, kv, rows, head_size), bf16),
                pltpu.VMEM((slots + 1, 2, rows, 128), f32),
                pltpu.VMEM((slots + 1, particles, kv, rows, head_size), bf16),
                pltpu.VMEM((slots + 1, 2, rows, 128), f32),
                pltpu.VMEM((kv, particles * rows, head_size), f32),
                pltpu.VMEM((1, depth * heads), f32),
                dma((2, n - 1)),
                dma((2, n - 1)),
                dma((2, max(chips - 1, 1))),
                dma((2, max(chips - 1, 1))),
                dma((2, chips)),
                dma((2, chips)),
            ]
            + [dma((slots, 2))] * 6,
            compiler_params=pltpu.CompilerParams(
                collective_id=1 + number, has_side_effects=True, vmem_limit_bytes=VMEM_LIMIT
            ),
        )(
            all_ids,
            owned,
            hot,
            norm_gain,
            jnp.asarray(own_bias(particles, steps, rows)),
            jnp.asarray(cosine),
            jnp.asarray(sine),
            w_query,
            w_key,
            w_value,
            key_cache,
            value_cache,
        )

    chosen = list(itertools.product(hubs, repeat=groups)) if hubs else []
    branches = [
        functools.partial(run, narrow, cap, pair, number) for number, pair in enumerate(chosen)
    ]
    full = {r: particles for r in range(1, n)}
    branches.append(functools.partial(run, full, None, None, len(chosen)))
    if not chosen:
        return branches[0]()
    return lax.switch(plan[0], branches)


def solution(mesh):
    in_specs = (
        P(("groups", "particle"), None),
        P(("groups", "particle")),
        P("particle", "head"),
        P(),
        P(None, "head"),
        P(None, "head"),
        P(None, "head"),
        P(("groups", "particle"), "head", None, None),
        P(("groups", "particle"), "head", None, None),
    )
    out_specs = P(("groups", "particle"), None, "head")
    return jax.shard_map(
        functools.partial(
            per_device, mesh.shape["groups"], mesh.shape["particle"], mesh.shape["head"]
        ),
        mesh=mesh,
        in_specs=in_specs,
        out_specs=out_specs,
        check_vma=False,
    )
```
